32 devices in a mesh: xy: 16 (over z, x, core), gz: 2 (over y).
Axes of the slice: x: 2, y: 2, z: 4, core: 2. Of those that a mesh axis runs over, the one named last changes fastest.
Arguments:
- conductivity: float32 [32, 256, 512], P('gz', 'xy'), may hold values from 0.5 to 2
- start_fields: float32 [4, 32, 256, 512], P(None, 'gz', 'xy'), may hold values from -6 to 6
- electrodes: int32 [3, 4, 64], replicated, may hold values from 0 to 511, as said below
- currents: float32 [4, 64], replicated, may hold values from -16 to 16
- pair_table: int32 [4, 2], replicated, may hold values from 0 to 1
- bounds: float32 [2], replicated, may hold values from 0.05 to 30, as said below
Outputs:
- potentials: float32 [4, 32, 256, 512], P(None, 'gz', 'xy')
- sensitivity: float32 [4, 32, 256, 512], P(None, 'gz', 'xy')
The draws below stay inside these ranges and needn't reach their ends.
Inputs may be any that keep to these rules, and one draw needn't show every extreme that they name: `electrodes`: each index lies inside the grid along its own dimension. `bounds`: the first entry is positive and the second exceeds the largest eigenvalue of A.
All inputs are finite; a program needn't handle non-finite values.
Results may differ from the reference program's by a relative error of at most 0.00021.
Values sent between devices are 32-bit elements; how exact they have to be, the bound alone decides.
A program may use at most 128 MiB of HBM per device.

```python
import math
import jax
import jax.numpy as jnp
from jax import lax

NY = 512
FIELDS = 4
PAIRS = 4
DEGREE = 4
SWEEPS = 2
NZ = 32
NX = 256
ELECTRODES = 64


def draw_electrodes(key, part):
    key = jax.random.fold_in(key, 11)
    keys = jax.random.split(key, 3)
    depth = jax.random.randint(keys[0], (FIELDS, ELECTRODES), 0, NZ)
    first = jax.random.randint(keys[1], (FIELDS, ELECTRODES), 0, NX)
    second = jax.random.randint(keys[2], (FIELDS, ELECTRODES), 0, NY)
    return jnp.stack([depth, first, second]).astype(jnp.int32)


def draw_bounds(key, part):
    key = jax.random.fold_in(key, 23)
    keys = jax.random.split(key, 2)
    lower = jax.random.uniform(keys[0], (1,), jnp.float32, 0.05, 0.2)
    upper = jax.random.uniform(keys[1], (1,), jnp.float32, 25.0, 30.0)
    return jnp.concatenate([lower, upper]).astype(jnp.float32)


def plant(entries, rng, low, largest):
    place = [jax.random.randint(jax.random.fold_in(rng, axis), (), 0, length) for axis, length in enumerate(entries.shape)]
    longest = entries.shape.index(max(entries.shape))
    neighbour = place[:longest] + [(place[longest] + 1) % entries.shape[longest]] + place[longest + 1:]
    return entries.at[tuple(place)].set(low).at[tuple(neighbour)].set(largest)


def steps_of(own_key, shape, pieces, low, largest):
    level = 1.0
    for axis_at, shards_of in pieces:
        draws = jax.random.uniform(jax.random.fold_in(jax.random.fold_in(own_key, 6), axis_at), (shards_of,), jnp.float32, low / len(pieces), largest / len(pieces))
        level = level * jnp.repeat(jnp.exp(draws), shape[axis_at] // shards_of).reshape((-1,) + (1,) * (len(shape) - 1 - axis_at))
    return level


def scatter_about(key, shape, width, most, pieces=(), kind=jnp.bfloat16):
    drawn = width * jax.random.normal(key, shape, jnp.float32)
    if pieces:
        drawn = drawn * steps_of(key, shape, pieces, -0.22, 0.18)
    return jnp.clip(drawn, -most, most).astype(kind)


def setup_inputs(seed: int = 0) -> dict:
    key_of = jax.random.split(jax.random.key(seed), 7)
    conductivity = jnp.clip(jnp.exp(math.log(2.0) - 1.3862944 * jax.random.uniform(key_of[0], (NZ, NX, NY), jnp.float32) ** steps_of(key_of[0], (NZ, NX, NY), ((0, 2), (1, 16)), -0.2, 0.2)), 0.5, 2.0)
    start_fields = scatter_about(key_of[1], (FIELDS, NZ, NX, NY), 1.0, 6.0, ((1, 2), (2, 16)), jnp.float32)
    electrodes = draw_electrodes(jax.random.fold_in(key_of[6], 71), 0)
    currents = scatter_about(key_of[3], (FIELDS, ELECTRODES), 4.0, 16.0, (), jnp.float32)
    pair_table = plant(jax.random.randint(key_of[4], (PAIRS, 2), 0, 2), jax.random.fold_in(key_of[4], 1), 0, 1).astype(jnp.int32)
    bounds = draw_bounds(jax.random.fold_in(key_of[6], 71), 0)
    return dict(conductivity=conductivity, start_fields=start_fields, electrodes=electrodes, currents=currents, pair_table=pair_table, bounds=bounds)


def prior_taps():
    raw = [(1.0 + math.sqrt(3.0) * abs(k) / 2.0) * math.exp(-math.sqrt(3.0) * abs(k) / 2.0) for k in range(-4, 5)]
    total = sum(raw)
    return [v / total for v in raw]

def shifted(array, axis, step):
    widths = [(0, 0)] * array.ndim
    widths[axis] = (1, 1)
    padded = jnp.pad(array, widths)
    return lax.slice_in_dim(padded, 1 + step, 1 + step + array.shape[axis], axis=axis)

def coefficients(conductivity):
    result = []
    for axis in range(3):
        for step in (-1, 1):
            result.append(0.5 * (conductivity + shifted(conductivity, axis, step)))
    return result

def operate(field, coefs):
    total = jnp.zeros_like(field)
    index = 0
    for axis in range(3):
        for step in (-1, 1):
            total = total + coefs[index][None] * (field - shifted(field, axis + 1, step))
            index = index + 1
    return total

def smooth(array, axis):
    taps = prior_taps()
    widths = [(0, 0)] * array.ndim
    widths[axis] = (4, 4)
    padded = jnp.pad(array, widths)
    length = array.shape[axis]
    total = jnp.zeros_like(array)
    for k in range(9):
        total = total + taps[k] * lax.slice_in_dim(padded, k, k + length, axis=axis)
    return total

def reference(conductivity, start_fields, electrodes, currents, pair_table, bounds):
    field_ids = jnp.broadcast_to(jnp.arange(FIELDS, dtype=jnp.int32)[:, None], currents.shape)
    rhs = jnp.zeros(start_fields.shape, jnp.float32).at[field_ids, electrodes[0], electrodes[1], electrodes[2]].add(currents)
    coefs = coefficients(conductivity)
    theta = 0.5 * (bounds[0] + bounds[1])
    delta = 0.5 * (bounds[1] - bounds[0])
    ratio = theta / delta
    state = start_fields
    for sweep in range(SWEEPS):
        resid = rhs - operate(state, coefs)
        direction = resid / theta
        rho = 1.0 / ratio
        for step in range(DEGREE):
            state = state + direction
            if step < DEGREE - 1:
                resid = resid - operate(direction, coefs)
                rho_new = 1.0 / (2.0 * ratio - rho)
                direction = rho_new * rho * direction + 2.0 * rho_new / delta * resid
                rho = rho_new
    sources = state[pair_table[:, 0]]
    receivers = state[2 + pair_table[:, 1]]
    raw = jnp.zeros(sources.shape, jnp.float32)
    for axis in range(1, 4):
        grad_s = 0.5 * (shifted(sources, axis, 1) - shifted(sources, axis, -1))
        grad_r = 0.5 * (shifted(receivers, axis, 1) - shifted(receivers, axis, -1))
        raw = raw + grad_s * grad_r
    raw = conductivity[None] * raw
    smoothed = smooth(smooth(smooth(raw, 3), 1), 2)
    return (state, smoothed)
```

```python
import functools
import math

import jax
import jax.numpy as jnp
import ml_dtypes
import numpy as np
from jax import lax
from jax.experimental import pallas as pl
from jax.experimental.pallas import tpu as pltpu
from jax.sharding import PartitionSpec as P

DEGREE = 4
SWEEPS = 2
REACH = 4
MESH = pl.DeviceIdType.MESH
F32 = jnp.float32
BF16 = jnp.bfloat16


def prior_taps():
    raw = [
        (1.0 + math.sqrt(3.0) * k / 2.0) * math.exp(-math.sqrt(3.0) * k / 2.0)
        for k in range(REACH + 1)
    ]
    total = raw[0] + 2.0 * sum(raw[1:])
    return [v / total for v in raw]


def split_taps():
    taps = np.asarray(prior_taps(), np.float32)
    high = taps.astype(ml_dtypes.bfloat16).astype(np.float32)
    return [float(v) for v in high], [float(v) for v in taps - high]


def band(distance, inside=None):
    parts = []
    for taps in split_taps():
        out = jnp.zeros(distance.shape, F32)
        for k in range(REACH + 1):
            hit = jnp.abs(distance) == k
            if inside is not None:
                hit = hit & inside
            out = jnp.where(hit, taps[k], out)
        parts.append(out.astype(BF16))
    return parts


def halves(a):
    high = a.astype(BF16)
    return high, (a - high.astype(F32)).astype(BF16)


def dot(a, b):
    return lax.dot_general(a, b, (((1,), (0,)), ((), ())), preferred_element_type=F32)


def kernel(
    pair_ref, bounds_ref, elec_ref, cur_ref, cond_hbm, start_hbm, pot_hbm, sens_hbm,
    cp, v, x, r, rowx, sfx, rcx, scx, cz, cxm, cxp, cym, cyp, cd, raw, u, w, xs, xr, sens, coef,
    ty, tc, te,
    load_sem, out_sem, send_sem, recv_sem, csend, crecv, zsend, zrecv, xsend, xrecv,
):
    fields, nz, nx, ny = x.shape
    pairs = u.shape[0]
    cells = nz * nx
    ix, iz = lax.axis_index("xy"), lax.axis_index("gz")
    has = [ix > 0, ix < lax.axis_size("xy") - 1, iz > 0, iz < lax.axis_size("gz") - 1]
    place = [
        (ix - 1, iz), (ix + 1, iz), (ix, iz - 1), (ix, iz + 1),
    ]

    barrier = pltpu.get_barrier_semaphore()
    loads = [pltpu.make_async_copy(cond_hbm, cp.at[pl.ds(1, nz)], load_sem.at[0])]
    for f in range(fields):
        loads.append(
            pltpu.make_async_copy(start_hbm.at[f], v.at[0, f, pl.ds(1, nz)], load_sem.at[1 + f])
        )
    loads.append(pltpu.make_async_copy(start_hbm, x, load_sem.at[1 + fields]))
    for copy in loads:
        copy.start()

    for d in range(4):
        @pl.when(jnp.logical_not(has[d]))
        def _():
            if d < 2:
                rcx[d] = jnp.zeros(rcx.shape[1:], F32)
                for slot in range(2):
                    for f in range(fields):
                        rowx[slot, f, d] = jnp.zeros(rowx.shape[3:], F32)
                for p in range(pairs):
                    xr[p, d] = jnp.zeros(xr.shape[2:], F32)
            else:
                edge = 0 if d == 2 else nz + 1
                cp[edge] = jnp.zeros((nx, ny), F32)
                for slot in range(2):
                    for f in range(fields):
                        v[slot, f, edge] = jnp.zeros((nx, ny), F32)
                first = 0 if d == 2 else nz + REACH
                for p in range(pairs):
                    u[p, first:first + REACH] = jnp.zeros((REACH, nx, ny), F32)

    for d in range(4):
        @pl.when(has[d])
        def _():
            pl.semaphore_signal(barrier, inc=1, device_id=place[d], device_id_type=MESH)
    pl.semaphore_wait(barrier, sum(h.astype(jnp.int32) for h in has))

    def field_copy(slot, f, d):
        o = d ^ 1
        if d < 2:
            src, dst = sfx.at[f, d], rowx.at[slot, f, o]
        else:
            src = v.at[slot, f, 1 if d == 2 else nz]
            dst = v.at[slot, f, nz + 1 if d == 2 else 0]
        return pltpu.make_async_remote_copy(
            src_ref=src, dst_ref=dst, send_sem=send_sem.at[f, d],
            recv_sem=recv_sem.at[slot, f, o], device_id=place[d], device_id_type=MESH,
        )

    def field_arrival(slot, f, d):
        if d < 2:
            src, dst = sfx.at[f, d], rowx.at[slot, f, d]
        else:
            src = v.at[slot, f, 1 if d == 2 else nz]
            dst = v.at[slot, f, 0 if d == 2 else nz + 1]
        return pltpu.make_async_remote_copy(
            src_ref=src, dst_ref=dst, send_sem=send_sem.at[f, d],
            recv_sem=recv_sem.at[slot, f, d], device_id=place[d], device_id_type=MESH,
        )

    def cond_copy(d, arrives):
        o = d if arrives else d ^ 1
        if d < 2:
            src, dst = scx.at[d], rcx.at[o]
        else:
            src = cp.at[1 if d == 2 else nz]
            dst = cp.at[0 if o == 2 else nz + 1]
        return pltpu.make_async_remote_copy(
            src_ref=src, dst_ref=dst, send_sem=csend.at[d], recv_sem=crecv.at[o],
            device_id=place[d], device_id_type=MESH,
        )

    def send_field(slot, f):
        for d in range(4):
            @pl.when(has[d])
            def _():
                field_copy(slot, f, d).start()

    def wait_field(slot, f):
        for d in range(4):
            @pl.when(has[d])
            def _():
                field_arrival(slot, f, d).wait_recv()
                field_copy(slot, f, d).wait_send()

    loads[0].wait()

    @pl.loop(0, nz)
    def _(z):
        scx[0, z] = cp[z + 1, 0:1, :]
        scx[1, z] = cp[z + 1, nx - 1:nx, :]

    for d in range(4):
        @pl.when(has[d])
        def _():
            cond_copy(d, False).start()
    for f in range(fields):
        loads[1 + f].wait()

        @pl.loop(0, nz)
        def _(z):
            sfx[f, 0, z] = v[0, f, z + 1, 0:1, :]
            sfx[f, 1, z] = v[0, f, z + 1, nx - 1:nx, :]

        send_field(0, f)

    low = jnp.full((1, ny), bounds_ref[0], F32)
    high = jnp.full((1, ny), bounds_ref[1], F32)
    theta = 0.5 * (low + high)
    delta = 0.5 * (high - low)
    ratio = theta / delta
    for sweep in range(SWEEPS):
        rho = 1.0 / ratio
        for k in range(DEGREE):
            j = sweep * DEGREE + k
            if k == 0:
                coef[j, 0] = jnp.zeros((1, ny), F32)
                coef[j, 1] = 1.0 / theta
            else:
                rho_new = 1.0 / (2.0 * ratio - rho)
                coef[j, 0] = rho_new * rho
                coef[j, 1] = 2.0 * rho_new / delta
                rho = rho_new

    count = cur_ref.shape[1]
    cell_ids = lax.broadcasted_iota(jnp.int32, (cells, count), 0)
    second_ids = lax.broadcasted_iota(jnp.int32, (ny, count), 0)
    for f in range(fields):
        lz = elec_ref[0, f:f + 1, :] - iz * nz
        lx = elec_ref[1, f:f + 1, :] - ix * nx
        inside = (lz >= 0) & (lz < nz) & (lx >= 0) & (lx < nx)
        code = jnp.where(inside, lz * nx + lx, -1)
        at_cell = cell_ids == code
        at_second = jnp.where(second_ids == elec_ref[2, f:f + 1, :], 1.0, 0.0).astype(BF16)
        rest = cur_ref[f:f + 1, :]
        terms = []
        for _ in range(3):
            part = rest.astype(BF16).astype(F32)
            rest = rest - part
            left = jnp.where(at_cell, part, 0.0).astype(BF16)
            terms.append(
                lax.dot_general(
                    left, at_second, (((1,), (1,)), ((), ())), preferred_element_type=F32
                )
            )
        r[f] = ((terms[2] + terms[1]) + terms[0]).reshape(nz, nx, ny)

    a = lax.broadcasted_iota(jnp.int32, (ny, ny), 0)
    b = lax.broadcasted_iota(jnp.int32, (ny, ny), 1)
    ty[0], ty[1] = band(a - b)
    a = lax.broadcasted_iota(jnp.int32, (cells, cells), 0)
    b = lax.broadcasted_iota(jnp.int32, (cells, cells), 1)
    tc[0], tc[1] = band(a % nx - b % nx, a // nx == b // nx)
    rim = nz * REACH
    a = lax.broadcasted_iota(jnp.int32, (cells, rim), 0)
    b = lax.broadcasted_iota(jnp.int32, (cells, rim), 1)
    same = a // nx == b // REACH
    te[0, 0], te[0, 1] = band(a % nx - (b % REACH - REACH), same)
    te[1, 0], te[1, 1] = band(a % nx - (b % REACH + nx), same)

    rows = lax.broadcasted_iota(jnp.int32, (nx, ny), 0)
    lanes = lax.broadcasted_iota(jnp.int32, (nx, ny), 1)

    def x_down(a, row):
        return jnp.where(rows == 0, row, pltpu.roll(a, 1, 0))

    def x_up(a, row):
        return jnp.where(rows == nx - 1, row, pltpu.roll(a, nx - 1, 0))

    for d in range(4):
        @pl.when(has[d])
        def _():
            cond_copy(d, True).wait_recv()
            cond_copy(d, False).wait_send()

    @pl.loop(0, nz)
    def _(z):
        c = cp[z + 1]
        half = 0.5 * c
        zm = half + 0.5 * cp[z]
        zp = half + 0.5 * cp[z + 2]
        xm = half + 0.5 * x_down(c, rcx[0, z])
        xp = half + 0.5 * x_up(c, rcx[1, z])
        ym = half + 0.5 * jnp.where(lanes == 0, 0.0, pltpu.roll(c, 1, 1))
        yp = half + 0.5 * jnp.where(lanes == ny - 1, 0.0, pltpu.roll(c, ny - 1, 1))
        cz[z] = zm
        cz[z + 1] = zp
        cxm[z] = xm
        cxp[z] = xp
        cym[z] = jnp.where(lanes == 0, 0.0, ym)
        cyp[z] = jnp.where(lanes == ny - 1, 0.0, yp)
        cd[z] = ((zm + zp) + (xm + xp)) + (ym + yp)

    loads[1 + fields].wait()

    def step(j, last):
        slot = lax.rem(j, 2)
        later = 1 - slot
        fac_d = coef[j, 0]
        fac_r = coef[j, 1]
        for f in range(fields):
            wait_field(slot, f)

            @pl.loop(0, nz, unroll=2)
            def _(z):
                c = v[slot, f, z + 1]
                total = cz[z] * v[slot, f, z] + cz[z + 1] * v[slot, f, z + 2]
                total = total + cxm[z] * x_down(c, rowx[slot, f, 0, z])
                total = total + cxp[z] * x_up(c, rowx[slot, f, 1, z])
                total = total + cym[z] * pltpu.roll(c, 1, 1)
                total = total + cyp[z] * pltpu.roll(c, ny - 1, 1)
                res = r[f, z] + (total - cd[z] * c)
                new = fac_d * c + fac_r * res
                at = x[f, z] + new
                if last:
                    new = at
                else:
                    r[f, z] = res
                    x[f, z] = at
                v[later, f, z + 1] = new
                sfx[f, 0, z] = new[0:1, :]
                sfx[f, 1, z] = new[nx - 1:nx, :]

            send_field(later, f)
            if last:
                pltpu.make_async_copy(
                    v.at[later, f, pl.ds(1, nz)], pot_hbm.at[f], out_sem.at[f]
                ).start()

    steps = SWEEPS * DEGREE
    end = steps % 2

    @pl.loop(0, steps - 1)
    def _(j):
        step(j, False)

    step(jnp.int32(steps - 1), True)

    for f in range(fields):
        wait_field(end, f)

    def z_copy(p, d, arrives):
        o = d if arrives else d ^ 1
        src = u.at[p, pl.ds(REACH if d == 2 else nz, REACH)]
        dst = u.at[p, pl.ds(0 if o == 2 else nz + REACH, REACH)]
        return pltpu.make_async_remote_copy(
            src_ref=src, dst_ref=dst, send_sem=zsend.at[p, d - 2], recv_sem=zrecv.at[p, o - 2],
            device_id=place[d], device_id_type=MESH,
        )

    def x_copy(p, d, arrives):
        o = d if arrives else d ^ 1
        return pltpu.make_async_remote_copy(
            src_ref=xs.at[p, d], dst_ref=xr.at[p, o], send_sem=xsend.at[p, d],
            recv_sem=xrecv.at[p, o], device_id=place[d], device_id_type=MESH,
        )

    def slope_x(f, z, c):
        return x_up(c, rowx[end, f, 1, z]) - x_down(c, rowx[end, f, 0, z])

    def slope_y(c):
        ahead = jnp.where(lanes == ny - 1, 0.0, pltpu.roll(c, ny - 1, 1))
        return ahead - jnp.where(lanes == 0, 0.0, pltpu.roll(c, 1, 1))

    for p in range(pairs):
        s = pair_ref[p, 0]
        q = pair_ref[p, 1] + 2

        @pl.loop(0, nz, unroll=2)
        def _(z):
            sc = v[end, s, z + 1]
            qc = v[end, q, z + 1]
            total = (v[end, s, z + 2] - v[end, s, z]) * (v[end, q, z + 2] - v[end, q, z])
            total = total + slope_x(s, z, sc) * slope_x(q, z, qc)
            total = total + slope_y(sc) * slope_y(qc)
            raw[z] = (0.25 * cp[z + 1]) * total

        rh, rl = halves(raw[...].reshape(cells, ny))
        smooth = (dot(rl, ty[0]) + dot(rh, ty[1])) + dot(rh, ty[0])
        u[p, REACH:REACH + nz] = smooth.reshape(nz, nx, ny)
        for d in (2, 3):
            @pl.when(has[d])
            def _():
                z_copy(p, d, False).start()

    taps = prior_taps()
    for p in range(pairs):
        for d in (2, 3):
            @pl.when(has[d])
            def _():
                z_copy(p, d, True).wait_recv()

        for z in range(nz):
            total = taps[0] * u[p, z + REACH]
            for k in range(1, REACH + 1):
                total = total + taps[k] * (u[p, z + REACH - k] + u[p, z + REACH + k])
            w[p, z] = total
            xs[p, 0, z * REACH:(z + 1) * REACH] = total[0:REACH]
            xs[p, 1, z * REACH:(z + 1) * REACH] = total[nx - REACH:nx]

        for d in (0, 1):
            @pl.when(has[d])
            def _():
                x_copy(p, d, False).start()

    for p in range(pairs):
        wh, wl = halves(w[p].reshape(cells, ny))
        total = (dot(tc[0], wl) + dot(tc[1], wh)) + dot(tc[0], wh)
        for d in (0, 1):
            @pl.when(has[d])
            def _():
                x_copy(p, d, True).wait_recv()
        for d in (0, 1):
            eh, el = halves(xr[p, d])
            total = total + ((dot(te[d, 0], el) + dot(te[d, 1], eh)) + dot(te[d, 0], eh))
        sens[p] = total.reshape(nz, nx, ny)
        pltpu.make_async_copy(sens.at[p], sens_hbm.at[p], out_sem.at[fields + p]).start()

    for p in range(pairs):
        for d in range(4):
            @pl.when(has[d])
            def _():
                (x_copy if d < 2 else z_copy)(p, d, False).wait_send()
        pltpu.make_async_copy(sens.at[p], sens_hbm.at[p], out_sem.at[fields + p]).wait()
    for f in range(fields):
        pltpu.make_async_copy(
            v.at[end, f, pl.ds(1, nz)], pot_hbm.at[f], out_sem.at[f]
        ).wait()


def local(conductivity, start_fields, electrodes, currents, pair_table, bounds):
    fields, nz, nx, ny = start_fields.shape
    pairs = pair_table.shape[0]
    steps = SWEEPS * DEGREE
    slab = (nz, nx, ny)
    smem = pl.BlockSpec(memory_space=pltpu.SMEM)
    vmem = pl.BlockSpec(memory_space=pltpu.VMEM)
    hbm = pl.BlockSpec(memory_space=pl.ANY)
    rim = nz * REACH
    scratch = [
        pltpu.VMEM((nz + 2, nx, ny), F32),
        pltpu.VMEM((2, fields, nz + 2, nx, ny), F32),
        pltpu.VMEM((fields,) + slab, F32),
        pltpu.VMEM((fields,) + slab, F32),
        pltpu.VMEM((2, fields, 2, nz, 1, ny), F32),
        pltpu.VMEM((fields, 2, nz, 1, ny), F32),
        pltpu.VMEM((2, nz, 1, ny), F32),
        pltpu.VMEM((2, nz, 1, ny), F32),
        pltpu.VMEM((nz + 1, nx, ny), F32),
        pltpu.VMEM(slab, F32),
        pltpu.VMEM(slab, F32),
        pltpu.VMEM(slab, F32),
        pltpu.VMEM(slab, F32),
        pltpu.VMEM(slab, F32),
        pltpu.VMEM(slab, F32),
        pltpu.VMEM((pairs, nz + 2 * REACH, nx, ny), F32),
        pltpu.VMEM((pairs,) + slab, F32),
        pltpu.VMEM((pairs, 2, rim, ny), F32),
        pltpu.VMEM((pairs, 2, rim, ny), F32),
        pltpu.VMEM((pairs,) + slab, F32),
        pltpu.VMEM((steps, 2, 1, ny), F32),
        pltpu.VMEM((2, ny, ny), BF16),
        pltpu.VMEM((2, nz * nx, nz * nx), BF16),
        pltpu.VMEM((2, 2, nz * nx, rim), BF16),
        pltpu.SemaphoreType.DMA((fields + 2,)),
        pltpu.SemaphoreType.DMA((fields + pairs,)),
        pltpu.SemaphoreType.DMA((fields, 4)),
        pltpu.SemaphoreType.DMA((2, fields, 4)),
        pltpu.SemaphoreType.DMA((4,)),
        pltpu.SemaphoreType.DMA((4,)),
        pltpu.SemaphoreType.DMA((pairs, 2)),
        pltpu.SemaphoreType.DMA((pairs, 2)),
        pltpu.SemaphoreType.DMA((pairs, 2)),
        pltpu.SemaphoreType.DMA((pairs, 2)),
    ]
    out = jax.ShapeDtypeStruct((fields,) + slab, F32)
    out_sens = jax.ShapeDtypeStruct((pairs,) + slab, F32)
    return pl.pallas_call(
        kernel,
        out_shape=(out, out_sens),
        in_specs=[smem, smem, vmem, vmem, hbm, hbm],
        out_specs=(hbm, hbm),
        scratch_shapes=scratch,
        compiler_params=pltpu.CompilerParams(
            collective_id=0, has_side_effects=True, vmem_limit_bytes=48 * 1024 * 1024
        ),
    )(pair_table, bounds, electrodes, currents, conductivity, start_fields)


def solution(mesh):
    placed = (P("gz", "xy", None), P(None, "gz", "xy", None), P(), P(), P(), P())
    return jax.shard_map(
        local,
        mesh=mesh,
        in_specs=placed,
        out_specs=(P(None, "gz", "xy", None), P(None, "gz", "xy", None)),
        check_vma=False,
    )
```

```python
import functools
import math

import jax
import jax.numpy as jnp
import ml_dtypes
import numpy as np
from jax import lax
from jax.experimental import pallas as pl
from jax.experimental.pallas import tpu as pltpu
from jax.sharding import PartitionSpec as P

DEGREE = 4
SWEEPS = 2
REACH = 4
MESH = pl.DeviceIdType.MESH
F32 = jnp.float32
BF16 = jnp.bfloat16


def prior_taps():
    raw = [
        (1.0 + math.sqrt(3.0) * k / 2.0) * math.exp(-math.sqrt(3.0) * k / 2.0)
        for k in range(REACH + 1)
    ]
    total = raw[0] + 2.0 * sum(raw[1:])
    return [v / total for v in raw]


def split_taps():
    taps = np.asarray(prior_taps(), np.float32)
    high = taps.astype(ml_dtypes.bfloat16).astype(np.float32)
    return [float(v) for v in high], [float(v) for v in taps - high]


def band(distance, inside=None):
    parts = []
    for taps in split_taps():
        out = jnp.zeros(distance.shape, F32)
        for k in range(REACH + 1):
            hit = jnp.abs(distance) == k
            if inside is not None:
                hit = hit & inside
            out = jnp.where(hit, taps[k], out)
        parts.append(out.astype(BF16))
    return parts


def halves(a):
    high = a.astype(BF16)
    return high, (a - high.astype(F32)).astype(BF16)


def dot(a, b):
    return lax.dot_general(a, b, (((1,), (0,)), ((), ())), preferred_element_type=F32)


def kernel(
    pair_ref, bounds_ref, elec_ref, cur_ref, cond_hbm, start_hbm, pot_hbm, sens_hbm,
    cp, v, x, r, rowx, sfx, rcx, scx, cz, cxm, cxp, cym, cyp, cd, raw, u, w, xs, xr, sens, coef,
    ty, tc, te,
    load_sem, out_sem, send_sem, recv_sem, csend, crecv, zsend, zrecv, xsend, xrecv,
):
    fields, nz, nx, ny = x.shape
    pairs = u.shape[0]
    cells = nz * nx
    ix, iz = lax.axis_index("xy"), lax.axis_index("gz")
    has = [ix > 0, ix < lax.axis_size("xy") - 1, iz > 0, iz < lax.axis_size("gz") - 1]
    place = [
        (ix - 1, iz), (ix + 1, iz), (ix, iz - 1), (ix, iz + 1),
    ]

    barrier = pltpu.get_barrier_semaphore()
    loads = [pltpu.make_async_copy(cond_hbm, cp.at[pl.ds(1, nz)], load_sem.at[0])]
    for f in range(fields):
        loads.append(
            pltpu.make_async_copy(start_hbm.at[f], v.at[0, f, pl.ds(1, nz)], load_sem.at[1 + f])
        )
    loads.append(pltpu.make_async_copy(start_hbm, x, load_sem.at[1 + fields]))
    for copy in loads:
        copy.start()

    for d in range(4):
        @pl.when(jnp.logical_not(has[d]))
        def _():
            if d < 2:
                rcx[d] = jnp.zeros(rcx.shape[1:], F32)
                for slot in range(2):
                    for f in range(fields):
                        rowx[slot, f, d] = jnp.zeros(rowx.shape[3:], F32)
                for p in range(pairs):
                    xr[p, d] = jnp.zeros(xr.shape[2:], F32)
            else:
                edge = 0 if d == 2 else nz + 1
                cp[edge] = jnp.zeros((nx, ny), F32)
                for slot in range(2):
                    for f in range(fields):
                        v[slot, f, edge] = jnp.zeros((nx, ny), F32)
                first = 0 if d == 2 else nz + REACH
                for p in range(pairs):
                    u[p, first:first + REACH] = jnp.zeros((REACH, nx, ny), F32)

    for d in range(4):
        @pl.when(has[d])
        def _():
            pl.semaphore_signal(barrier, inc=1, device_id=place[d], device_id_type=MESH)
    pl.semaphore_wait(barrier, sum(h.astype(jnp.int32) for h in has))

    def field_copy(slot, f, d):
        o = d ^ 1
        if d < 2:
            src, dst = sfx.at[f, d], rowx.at[slot, f, o]
        else:
            src = v.at[slot, f, 1 if d == 2 else nz]
            dst = v.at[slot, f, nz + 1 if d == 2 else 0]
        return pltpu.make_async_remote_copy(
            src_ref=src, dst_ref=dst, send_sem=send_sem.at[f, d],
            recv_sem=recv_sem.at[slot, f, o], device_id=place[d], device_id_type=MESH,
        )

    def field_arrival(slot, f, d):
        if d < 2:
            src, dst = sfx.at[f, d], rowx.at[slot, f, d]
        else:
            src = v.at[slot, f, 1 if d == 2 else nz]
            dst = v.at[slot, f, 0 if d == 2 else nz + 1]
        return pltpu.make_async_remote_copy(
            src_ref=src, dst_ref=dst, send_sem=send_sem.at[f, d],
            recv_sem=recv_sem.at[slot, f, d], device_id=place[d], device_id_type=MESH,
        )

    def cond_copy(d, arrives):
        o = d if arrives else d ^ 1
        if d < 2:
            src, dst = scx.at[d], rcx.at[o]
        else:
            src = cp.at[1 if d == 2 else nz]
            dst = cp.at[0 if o == 2 else nz + 1]
        return pltpu.make_async_remote_copy(
            src_ref=src, dst_ref=dst, send_sem=csend.at[d], recv_sem=crecv.at[o],
            device_id=place[d], device_id_type=MESH,
        )

    def send_field(slot, f):
        for d in range(4):
            @pl.when(has[d])
            def _():
                field_copy(slot, f, d).start()

    def wait_field(slot, f):
        for d in range(4):
            @pl.when(has[d])
            def _():
                field_arrival(slot, f, d).wait_recv()
                field_copy(slot, f, d).wait_send()

    loads[0].wait()

    @pl.loop(0, nz)
    def _(z):
        scx[0, z] = cp[z + 1, 0:1, :]
        scx[1, z] = cp[z + 1, nx - 1:nx, :]

    for d in range(4):
        @pl.when(has[d])
        def _():
            cond_copy(d, False).start()
    for f in range(fields):
        loads[1 + f].wait()

        @pl.loop(0, nz)
        def _(z):
            sfx[f, 0, z] = v[0, f, z + 1, 0:1, :]
            sfx[f, 1, z] = v[0, f, z + 1, nx - 1:nx, :]

        send_field(0, f)

    low = jnp.full((1, ny), bounds_ref[0], F32)
    high = jnp.full((1, ny), bounds_ref[1], F32)
    theta = 0.5 * (low + high)
    delta = 0.5 * (high - low)
    ratio = theta / delta
    for sweep in range(SWEEPS):
        rho = 1.0 / ratio
        for k in range(DEGREE):
            j = sweep * DEGREE + k
            if k == 0:
                coef[j, 0] = jnp.zeros((1, ny), F32)
                coef[j, 1] = 1.0 / theta
            else:
                rho_new = 1.0 / (2.0 * ratio - rho)
                coef[j, 0] = rho_new * rho
                coef[j, 1] = 2.0 * rho_new / delta
                rho = rho_new

    count = cur_ref.shape[1]
    cell_ids = lax.broadcasted_iota(jnp.int32, (cells, count), 0)
    second_ids = lax.broadcasted_iota(jnp.int32, (ny, count), 0)
    for f in range(fields):
        lz = elec_ref[0, f:f + 1, :] - iz * nz
        lx = elec_ref[1, f:f + 1, :] - ix * nx
        inside = (lz >= 0) & (lz < nz) & (lx >= 0) & (lx < nx)
        code = jnp.where(inside, lz * nx + lx, -1)
        at_cell = cell_ids == code
        at_second = jnp.where(second_ids == elec_ref[2, f:f + 1, :], 1.0, 0.0).astype(BF16)
        rest = cur_ref[f:f + 1, :]
        terms = []
        for _ in range(3):
            part = rest.astype(BF16).astype(F32)
            rest = rest - part
            left = jnp.where(at_cell, part, 0.0).astype(BF16)
            terms.append(
                lax.dot_general(
                    left, at_second, (((1,), (1,)), ((), ())), preferred_element_type=F32
                )
            )
        r[f] = ((terms[2] + terms[1]) + terms[0]).reshape(nz, nx, ny)

    a = lax.broadcasted_iota(jnp.int32, (ny, ny), 0)
    b = lax.broadcasted_iota(jnp.int32, (ny, ny), 1)
    ty[0], ty[1] = band(a - b)
    a = lax.broadcasted_iota(jnp.int32, (cells, cells), 0)
    b = lax.broadcasted_iota(jnp.int32, (cells, cells), 1)
    tc[0], tc[1] = band(a % nx - b % nx, a // nx == b // nx)
    rim = nz * REACH
    a = lax.broadcasted_iota(jnp.int32, (cells, rim), 0)
    b = lax.broadcasted_iota(jnp.int32, (cells, rim), 1)
    same = a // nx == b // REACH
    te[0, 0], te[0, 1] = band(a % nx - (b % REACH - REACH), same)
    te[1, 0], te[1, 1] = band(a % nx - (b % REACH + nx), same)

    rows = lax.broadcasted_iota(jnp.int32, (nx, ny), 0)
    lanes = lax.broadcasted_iota(jnp.int32, (nx, ny), 1)

    def x_down(a, row):
        return jnp.where(rows == 0, row, pltpu.roll(a, 1, 0))

    def x_up(a, row):
        return jnp.where(rows == nx - 1, row, pltpu.roll(a, nx - 1, 0))

    for d in range(4):
        @pl.when(has[d])
        def _():
            cond_copy(d, True).wait_recv()
            cond_copy(d, False).wait_send()

    @pl.loop(0, nz, unroll=nz)
    def _(z):
        c = cp[z + 1]
        half = 0.5 * c
        zm = half + 0.5 * cp[z]
        zp = half + 0.5 * cp[z + 2]
        xm = half + 0.5 * x_down(c, rcx[0, z])
        xp = half + 0.5 * x_up(c, rcx[1, z])
        ym = half + 0.5 * jnp.where(lanes == 0, 0.0, pltpu.roll(c, 1, 1))
        yp = half + 0.5 * jnp.where(lanes == ny - 1, 0.0, pltpu.roll(c, ny - 1, 1))
        cz[z] = zm
        cz[z + 1] = zp
        cxm[z] = xm
        cxp[z] = xp
        cym[z] = jnp.where(lanes == 0, 0.0, ym)
        cyp[z] = jnp.where(lanes == ny - 1, 0.0, yp)
        cd[z] = ((zm + zp) + (xm + xp)) + (ym + yp)

    loads[1 + fields].wait()

    def step(j, last):
        slot = lax.rem(j, 2)
        later = 1 - slot
        fac_d = coef[j, 0]
        fac_r = coef[j, 1]
        for f in range(fields):
            wait_field(slot, f)

            @pl.loop(0, nz, unroll=nz)
            def _(z):
                c = v[slot, f, z + 1]
                total = cz[z] * v[slot, f, z] + cz[z + 1] * v[slot, f, z + 2]
                total = total + cxm[z] * x_down(c, rowx[slot, f, 0, z])
                total = total + cxp[z] * x_up(c, rowx[slot, f, 1, z])
                total = total + cym[z] * pltpu.roll(c, 1, 1)
                total = total + cyp[z] * pltpu.roll(c, ny - 1, 1)
                res = r[f, z] + (total - cd[z] * c)
                new = fac_d * c + fac_r * res
                at = x[f, z] + new
                if last:
                    new = at
                else:
                    r[f, z] = res
                    x[f, z] = at
                v[later, f, z + 1] = new
                sfx[f, 0, z] = new[0:1, :]
                sfx[f, 1, z] = new[nx - 1:nx, :]

            send_field(later, f)
            if last:
                pltpu.make_async_copy(
                    v.at[later, f, pl.ds(1, nz)], pot_hbm.at[f], out_sem.at[f]
                ).start()

    steps = SWEEPS * DEGREE
    end = steps % 2

    @pl.loop(0, steps - 1)
    def _(j):
        step(j, False)

    step(jnp.int32(steps - 1), True)

    for f in range(fields):
        wait_field(end, f)

    def z_copy(p, d, arrives):
        o = d if arrives else d ^ 1
        src = u.at[p, pl.ds(REACH if d == 2 else nz, REACH)]
        dst = u.at[p, pl.ds(0 if o == 2 else nz + REACH, REACH)]
        return pltpu.make_async_remote_copy(
            src_ref=src, dst_ref=dst, send_sem=zsend.at[p, d - 2], recv_sem=zrecv.at[p, o - 2],
            device_id=place[d], device_id_type=MESH,
        )

    def x_copy(p, d, arrives):
        o = d if arrives else d ^ 1
        return pltpu.make_async_remote_copy(
            src_ref=xs.at[p, d], dst_ref=xr.at[p, o], send_sem=xsend.at[p, d],
            recv_sem=xrecv.at[p, o], device_id=place[d], device_id_type=MESH,
        )

    def slope_x(f, z, c):
        return x_up(c, rowx[end, f, 1, z]) - x_down(c, rowx[end, f, 0, z])

    def slope_y(c):
        ahead = jnp.where(lanes == ny - 1, 0.0, pltpu.roll(c, ny - 1, 1))
        return ahead - jnp.where(lanes == 0, 0.0, pltpu.roll(c, 1, 1))

    for p in range(pairs):
        s = pair_ref[p, 0]
        q = pair_ref[p, 1] + 2

        @pl.loop(0, nz, unroll=nz)
        def _(z):
            sc = v[end, s, z + 1]
            qc = v[end, q, z + 1]
            total = (v[end, s, z + 2] - v[end, s, z]) * (v[end, q, z + 2] - v[end, q, z])
            total = total + slope_x(s, z, sc) * slope_x(q, z, qc)
            total = total + slope_y(sc) * slope_y(qc)
            raw[z] = (0.25 * cp[z + 1]) * total

        rh, rl = halves(raw[...].reshape(cells, ny))
        smooth = (dot(rl, ty[0]) + dot(rh, ty[1])) + dot(rh, ty[0])
        u[p, REACH:REACH + nz] = smooth.reshape(nz, nx, ny)
        for d in (2, 3):
            @pl.when(has[d])
            def _():
                z_copy(p, d, False).start()

    taps = prior_taps()
    for p in range(pairs):
        for d in (2, 3):
            @pl.when(has[d])
            def _():
                z_copy(p, d, True).wait_recv()

        for z in range(nz):
            total = taps[0] * u[p, z + REACH]
            for k in range(1, REACH + 1):
                total = total + taps[k] * (u[p, z + REACH - k] + u[p, z + REACH + k])
            w[p, z] = total
            xs[p, 0, z * REACH:(z + 1) * REACH] = total[0:REACH]
            xs[p, 1, z * REACH:(z + 1) * REACH] = total[nx - REACH:nx]

        for d in (0, 1):
            @pl.when(has[d])
            def _():
                x_copy(p, d, False).start()

    for p in range(pairs):
        wh, wl = halves(w[p].reshape(cells, ny))
        total = (dot(tc[0], wl) + dot(tc[1], wh)) + dot(tc[0], wh)
        for d in (0, 1):
            @pl.when(has[d])
            def _():
                x_copy(p, d, True).wait_recv()
        for d in (0, 1):
            eh, el = halves(xr[p, d])
            total = total + ((dot(te[d, 0], el) + dot(te[d, 1], eh)) + dot(te[d, 0], eh))
        sens[p] = total.reshape(nz, nx, ny)
        pltpu.make_async_copy(sens.at[p], sens_hbm.at[p], out_sem.at[fields + p]).start()

    for p in range(pairs):
        for d in range(4):
            @pl.when(has[d])
            def _():
                (x_copy if d < 2 else z_copy)(p, d, False).wait_send()
        pltpu.make_async_copy(sens.at[p], sens_hbm.at[p], out_sem.at[fields + p]).wait()
    for f in range(fields):
        pltpu.make_async_copy(
            v.at[end, f, pl.ds(1, nz)], pot_hbm.at[f], out_sem.at[f]
        ).wait()


def local(conductivity, start_fields, electrodes, currents, pair_table, bounds):
    fields, nz, nx, ny = start_fields.shape
    pairs = pair_table.shape[0]
    steps = SWEEPS * DEGREE
    slab = (nz, nx, ny)
    smem = pl.BlockSpec(memory_space=pltpu.SMEM)
    vmem = pl.BlockSpec(memory_space=pltpu.VMEM)
    hbm = pl.BlockSpec(memory_space=pl.ANY)
    rim = nz * REACH
    scratch = [
        pltpu.VMEM((nz + 2, nx, ny), F32),
        pltpu.VMEM((2, fields, nz + 2, nx, ny), F32),
        pltpu.VMEM((fields,) + slab, F32),
        pltpu.VMEM((fields,) + slab, F32),
        pltpu.VMEM((2, fields, 2, nz, 1, ny), F32),
        pltpu.VMEM((fields, 2, nz, 1, ny), F32),
        pltpu.VMEM((2, nz, 1, ny), F32),
        pltpu.VMEM((2, nz, 1, ny), F32),
        pltpu.VMEM((nz + 1, nx, ny), F32),
        pltpu.VMEM(slab, F32),
        pltpu.VMEM(slab, F32),
        pltpu.VMEM(slab, F32),
        pltpu.VMEM(slab, F32),
        pltpu.VMEM(slab, F32),
        pltpu.VMEM(slab, F32),
        pltpu.VMEM((pairs, nz + 2 * REACH, nx, ny), F32),
        pltpu.VMEM((pairs,) + slab, F32),
        pltpu.VMEM((pairs, 2, rim, ny), F32),
        pltpu.VMEM((pairs, 2, rim, ny), F32),
        pltpu.VMEM((pairs,) + slab, F32),
        pltpu.VMEM((steps, 2, 1, ny), F32),
        pltpu.VMEM((2, ny, ny), BF16),
        pltpu.VMEM((2, nz * nx, nz * nx), BF16),
        pltpu.VMEM((2, 2, nz * nx, rim), BF16),
        pltpu.SemaphoreType.DMA((fields + 2,)),
        pltpu.SemaphoreType.DMA((fields + pairs,)),
        pltpu.SemaphoreType.DMA((fields, 4)),
        pltpu.SemaphoreType.DMA((2, fields, 4)),
        pltpu.SemaphoreType.DMA((4,)),
        pltpu.SemaphoreType.DMA((4,)),
        pltpu.SemaphoreType.DMA((pairs, 2)),
        pltpu.SemaphoreType.DMA((pairs, 2)),
        pltpu.SemaphoreType.DMA((pairs, 2)),
        pltpu.SemaphoreType.DMA((pairs, 2)),
    ]
    out = jax.ShapeDtypeStruct((fields,) + slab, F32)
    out_sens = jax.ShapeDtypeStruct((pairs,) + slab, F32)
    return pl.pallas_call(
        kernel,
        out_shape=(out, out_sens),
        in_specs=[smem, smem, vmem, vmem, hbm, hbm],
        out_specs=(hbm, hbm),
        scratch_shapes=scratch,
        compiler_params=pltpu.CompilerParams(
            collective_id=0, has_side_effects=True, vmem_limit_bytes=48 * 1024 * 1024
        ),
    )(pair_table, bounds, electrodes, currents, conductivity, start_fields)


def solution(mesh):
    placed = (P("gz", "xy", None), P(None, "gz", "xy", None), P(), P(), P(), P())
    return jax.shard_map(
        local,
        mesh=mesh,
        in_specs=placed,
        out_specs=(P(None, "gz", "xy", None), P(None, "gz", "xy", None)),
        check_vma=False,
    )
```

```python
import functools
import math

import jax
import jax.numpy as jnp
import ml_dtypes
import numpy as np
from jax import lax
from jax.experimental import pallas as pl
from jax.experimental.pallas import tpu as pltpu
from jax.sharding import PartitionSpec as P

DEGREE = 4
SWEEPS = 2
REACH = 4
MESH = pl.DeviceIdType.MESH
F32 = jnp.float32
BF16 = jnp.bfloat16


def prior_taps():
    raw = [
        (1.0 + math.sqrt(3.0) * k / 2.0) * math.exp(-math.sqrt(3.0) * k / 2.0)
        for k in range(REACH + 1)
    ]
    total = raw[0] + 2.0 * sum(raw[1:])
    return [v / total for v in raw]


def split_taps():
    taps = np.asarray(prior_taps(), np.float32)
    high = taps.astype(ml_dtypes.bfloat16).astype(np.float32)
    return [float(v) for v in high], [float(v) for v in taps - high]


def band(distance, inside=None):
    parts = []
    for taps in split_taps():
        out = jnp.zeros(distance.shape, F32)
        for k in range(REACH + 1):
            hit = jnp.abs(distance) == k
            if inside is not None:
                hit = hit & inside
            out = jnp.where(hit, taps[k], out)
        parts.append(out.astype(BF16))
    return parts


def halves(a):
    high = a.astype(BF16)
    return high, (a - high.astype(F32)).astype(BF16)


def dot(a, b):
    return lax.dot_general(a, b, (((1,), (0,)), ((), ())), preferred_element_type=F32)


def kernel(
    pair_hbm, bounds_hbm, elec_hbm, cur_hbm, cond_hbm, start_hbm, pot_hbm, sens_hbm,
    pair_ref, bounds_ref, elec_ref, cur_ref,
    cp, v, x, r, rowx, sfx, rcx, scx, cz, cxm, cxp, cym, cyp, cd, raw, u, w, xs, xr, sens, coef,
    ty, tc, te,
    load_sem, small_sem, out_sem, send_sem, recv_sem, csend, crecv, zsend, zrecv, xsend, xrecv,
):
    fields, nz, nx, ny = x.shape
    pairs = u.shape[0]
    cells = nz * nx
    ix, iz = lax.axis_index("xy"), lax.axis_index("gz")
    has = [ix > 0, ix < lax.axis_size("xy") - 1, iz > 0, iz < lax.axis_size("gz") - 1]
    place = [
        (ix - 1, iz), (ix + 1, iz), (ix, iz - 1), (ix, iz + 1),
    ]

    barrier = pltpu.get_barrier_semaphore()
    loads = [pltpu.make_async_copy(cond_hbm, cp.at[pl.ds(1, nz)], load_sem.at[0])]
    for f in range(fields):
        loads.append(
            pltpu.make_async_copy(start_hbm.at[f], v.at[0, f, pl.ds(1, nz)], load_sem.at[1 + f])
        )
    loads.append(pltpu.make_async_copy(start_hbm, x, load_sem.at[1 + fields]))
    small = [
        pltpu.make_async_copy(src, dst, small_sem.at[i])
        for i, (src, dst) in enumerate([
            (pair_hbm, pair_ref), (bounds_hbm, bounds_ref), (elec_hbm, elec_ref),
            (cur_hbm, cur_ref),
        ])
    ]
    for copy in loads + small:
        copy.start()

    for d in range(4):
        @pl.when(jnp.logical_not(has[d]))
        def _():
            if d < 2:
                rcx[d] = jnp.zeros(rcx.shape[1:], F32)
                for slot in range(2):
                    for f in range(fields):
                        rowx[slot, f, d] = jnp.zeros(rowx.shape[3:], F32)
                for p in range(pairs):
                    xr[p, d] = jnp.zeros(xr.shape[2:], F32)
            else:
                edge = 0 if d == 2 else nz + 1
                cp[edge] = jnp.zeros((nx, ny), F32)
                for slot in range(2):
                    for f in range(fields):
                        v[slot, f, edge] = jnp.zeros((nx, ny), F32)
                first = 0 if d == 2 else nz + REACH
                for p in range(pairs):
                    u[p, first:first + REACH] = jnp.zeros((REACH, nx, ny), F32)

    for d in range(4):
        @pl.when(has[d])
        def _():
            pl.semaphore_signal(barrier, inc=1, device_id=place[d], device_id_type=MESH)
    pl.semaphore_wait(barrier, sum(h.astype(jnp.int32) for h in has))

    def field_copy(slot, f, d):
        o = d ^ 1
        if d < 2:
            src, dst = sfx.at[f, d], rowx.at[slot, f, o]
        else:
            src = v.at[slot, f, 1 if d == 2 else nz]
            dst = v.at[slot, f, nz + 1 if d == 2 else 0]
        return pltpu.make_async_remote_copy(
            src_ref=src, dst_ref=dst, send_sem=send_sem.at[f, d],
            recv_sem=recv_sem.at[slot, f, o], device_id=place[d], device_id_type=MESH,
        )

    def field_arrival(slot, f, d):
        if d < 2:
            src, dst = sfx.at[f, d], rowx.at[slot, f, d]
        else:
            src = v.at[slot, f, 1 if d == 2 else nz]
            dst = v.at[slot, f, 0 if d == 2 else nz + 1]
        return pltpu.make_async_remote_copy(
            src_ref=src, dst_ref=dst, send_sem=send_sem.at[f, d],
            recv_sem=recv_sem.at[slot, f, d], device_id=place[d], device_id_type=MESH,
        )

    def cond_copy(d, arrives):
        o = d if arrives else d ^ 1
        if d < 2:
            src, dst = scx.at[d], rcx.at[o]
        else:
            src = cp.at[1 if d == 2 else nz]
            dst = cp.at[0 if o == 2 else nz + 1]
        return pltpu.make_async_remote_copy(
            src_ref=src, dst_ref=dst, send_sem=csend.at[d], recv_sem=crecv.at[o],
            device_id=place[d], device_id_type=MESH,
        )

    def send_field(slot, f):
        for d in range(4):
            @pl.when(has[d])
            def _():
                field_copy(slot, f, d).start()

    def wait_field(slot, f):
        for d in range(4):
            @pl.when(has[d])
            def _():
                field_arrival(slot, f, d).wait_recv()
                field_copy(slot, f, d).wait_send()

    loads[0].wait()

    @pl.loop(0, nz)
    def _(z):
        scx[0, z] = cp[z + 1, 0:1, :]
        scx[1, z] = cp[z + 1, nx - 1:nx, :]

    for d in range(4):
        @pl.when(has[d])
        def _():
            cond_copy(d, False).start()
    for f in range(fields):
        loads[1 + f].wait()

        @pl.loop(0, nz)
        def _(z):
            sfx[f, 0, z] = v[0, f, z + 1, 0:1, :]
            sfx[f, 1, z] = v[0, f, z + 1, nx - 1:nx, :]

        send_field(0, f)

    for copy in small:
        copy.wait()

    low = jnp.full((1, ny), bounds_ref[0], F32)
    high = jnp.full((1, ny), bounds_ref[1], F32)
    theta = 0.5 * (low + high)
    delta = 0.5 * (high - low)
    ratio = theta / delta
    for sweep in range(SWEEPS):
        rho = 1.0 / ratio
        for k in range(DEGREE):
            j = sweep * DEGREE + k
            if k == 0:
                coef[j, 0] = jnp.zeros((1, ny), F32)
                coef[j, 1] = 1.0 / theta
            else:
                rho_new = 1.0 / (2.0 * ratio - rho)
                coef[j, 0] = rho_new * rho
                coef[j, 1] = 2.0 * rho_new / delta
                rho = rho_new

    count = cur_ref.shape[1]
    cell_ids = lax.broadcasted_iota(jnp.int32, (cells, count), 0)
    second_ids = lax.broadcasted_iota(jnp.int32, (ny, count), 0)
    for f in range(fields):
        lz = elec_ref[0, f:f + 1, :] - iz * nz
        lx = elec_ref[1, f:f + 1, :] - ix * nx
        inside = (lz >= 0) & (lz < nz) & (lx >= 0) & (lx < nx)
        code = jnp.where(inside, lz * nx + lx, -1)
        at_cell = cell_ids == code
        at_second = jnp.where(second_ids == elec_ref[2, f:f + 1, :], 1.0, 0.0).astype(BF16)
        rest = cur_ref[f:f + 1, :]
        terms = []
        for _ in range(3):
            part = rest.astype(BF16).astype(F32)
            rest = rest - part
            left = jnp.where(at_cell, part, 0.0).astype(BF16)
            terms.append(
                lax.dot_general(
                    left, at_second, (((1,), (1,)), ((), ())), preferred_element_type=F32
                )
            )
        r[f] = ((terms[2] + terms[1]) + terms[0]).reshape(nz, nx, ny)

    a = lax.broadcasted_iota(jnp.int32, (ny, ny), 0)
    b = lax.broadcasted_iota(jnp.int32, (ny, ny), 1)
    ty[0], ty[1] = band(a - b)
    a = lax.broadcasted_iota(jnp.int32, (cells, cells), 0)
    b = lax.broadcasted_iota(jnp.int32, (cells, cells), 1)
    tc[0], tc[1] = band(a % nx - b % nx, a // nx == b // nx)
    rim = nz * REACH
    a = lax.broadcasted_iota(jnp.int32, (cells, rim), 0)
    b = lax.broadcasted_iota(jnp.int32, (cells, rim), 1)
    same = a // nx == b // REACH
    te[0, 0], te[0, 1] = band(a % nx - (b % REACH - REACH), same)
    te[1, 0], te[1, 1] = band(a % nx - (b % REACH + nx), same)

    rows = lax.broadcasted_iota(jnp.int32, (nx, ny), 0)
    lanes = lax.broadcasted_iota(jnp.int32, (nx, ny), 1)

    def x_down(a, row):
        return jnp.where(rows == 0, row, pltpu.roll(a, 1, 0))

    def x_up(a, row):
        return jnp.where(rows == nx - 1, row, pltpu.roll(a, nx - 1, 0))

    for d in range(4):
        @pl.when(has[d])
        def _():
            cond_copy(d, True).wait_recv()
            cond_copy(d, False).wait_send()

    @pl.loop(0, nz, unroll=nz)
    def _(z):
        c = cp[z + 1]
        half = 0.5 * c
        zm = half + 0.5 * cp[z]
        zp = half + 0.5 * cp[z + 2]
        xm = half + 0.5 * x_down(c, rcx[0, z])
        xp = half + 0.5 * x_up(c, rcx[1, z])
        ym = half + 0.5 * jnp.where(lanes == 0, 0.0, pltpu.roll(c, 1, 1))
        yp = half + 0.5 * jnp.where(lanes == ny - 1, 0.0, pltpu.roll(c, ny - 1, 1))
        cz[z] = zm
        cz[z + 1] = zp
        cxm[z] = xm
        cxp[z] = xp
        cym[z] = jnp.where(lanes == 0, 0.0, ym)
        cyp[z] = jnp.where(lanes == ny - 1, 0.0, yp)
        cd[z] = ((zm + zp) + (xm + xp)) + (ym + yp)

    loads[1 + fields].wait()

    def step(j, last):
        slot = lax.rem(j, 2)
        later = 1 - slot
        fac_d = coef[j, 0]
        fac_r = coef[j, 1]
        for f in range(fields):
            wait_field(slot, f)

            @pl.loop(0, nz, unroll=nz)
            def _(z):
                c = v[slot, f, z + 1]
                total = cz[z] * v[slot, f, z] + cz[z + 1] * v[slot, f, z + 2]
                total = total + cxm[z] * x_down(c, rowx[slot, f, 0, z])
                total = total + cxp[z] * x_up(c, rowx[slot, f, 1, z])
                total = total + cym[z] * pltpu.roll(c, 1, 1)
                total = total + cyp[z] * pltpu.roll(c, ny - 1, 1)
                res = r[f, z] + (total - cd[z] * c)
                new = fac_d * c + fac_r * res
                at = x[f, z] + new
                if last:
                    new = at
                else:
                    r[f, z] = res
                    x[f, z] = at
                v[later, f, z + 1] = new
                sfx[f, 0, z] = new[0:1, :]
                sfx[f, 1, z] = new[nx - 1:nx, :]

            send_field(later, f)
            if last:
                pltpu.make_async_copy(
                    v.at[later, f, pl.ds(1, nz)], pot_hbm.at[f], out_sem.at[f]
                ).start()

    steps = SWEEPS * DEGREE
    end = steps % 2

    @pl.loop(0, steps - 1)
    def _(j):
        step(j, False)

    step(jnp.int32(steps - 1), True)

    for f in range(fields):
        wait_field(end, f)

    def z_copy(p, d, arrives):
        o = d if arrives else d ^ 1
        src = u.at[p, pl.ds(REACH if d == 2 else nz, REACH)]
        dst = u.at[p, pl.ds(0 if o == 2 else nz + REACH, REACH)]
        return pltpu.make_async_remote_copy(
            src_ref=src, dst_ref=dst, send_sem=zsend.at[p, d - 2], recv_sem=zrecv.at[p, o - 2],
            device_id=place[d], device_id_type=MESH,
        )

    def x_copy(p, d, arrives):
        o = d if arrives else d ^ 1
        return pltpu.make_async_remote_copy(
            src_ref=xs.at[p, d], dst_ref=xr.at[p, o], send_sem=xsend.at[p, d],
            recv_sem=xrecv.at[p, o], device_id=place[d], device_id_type=MESH,
        )

    def slope_x(f, z, c):
        return x_up(c, rowx[end, f, 1, z]) - x_down(c, rowx[end, f, 0, z])

    def slope_y(c):
        ahead = jnp.where(lanes == ny - 1, 0.0, pltpu.roll(c, ny - 1, 1))
        return ahead - jnp.where(lanes == 0, 0.0, pltpu.roll(c, 1, 1))

    def send_depth(p, values):
        u[p, REACH:REACH + nz] = values
        for d in (2, 3):
            @pl.when(has[d])
            def _():
                z_copy(p, d, False).start()

    def send_tiles(p):
        for z in range(nz):
            values = w[p, z]
            xs[p, 0, z * REACH:(z + 1) * REACH] = values[0:REACH]
            xs[p, 1, z * REACH:(z + 1) * REACH] = values[nx - REACH:nx]
        for d in (0, 1):
            @pl.when(has[d])
            def _():
                x_copy(p, d, False).start()

    taps = prior_taps()

    def smooth_depth(p, out):
        for d in (2, 3):
            @pl.when(has[d])
            def _():
                z_copy(p, d, True).wait_recv()
        for z in range(nz):
            total = taps[0] * u[p, z + REACH]
            for k in range(1, REACH + 1):
                total = total + taps[k] * (u[p, z + REACH - k] + u[p, z + REACH + k])
            out[p, z] = total

    def smooth_tiles(p):
        wh, wl = halves(w[p].reshape(cells, ny))
        total = (dot(tc[0], wl) + dot(tc[1], wh)) + dot(tc[0], wh)
        for d in (0, 1):
            @pl.when(has[d])
            def _():
                x_copy(p, d, True).wait_recv()
        for d in (0, 1):
            eh, el = halves(xr[p, d])
            total = total + ((dot(te[d, 0], el) + dot(te[d, 1], eh)) + dot(te[d, 0], eh))
        return total.reshape(nz, nx, ny)

    for p in range(pairs):
        s = pair_ref[p, 0]
        q = pair_ref[p, 1] + 2

        @pl.loop(0, nz, unroll=nz)
        def _(z):
            sc = v[end, s, z + 1]
            qc = v[end, q, z + 1]
            total = (v[end, s, z + 2] - v[end, s, z]) * (v[end, q, z + 2] - v[end, q, z])
            total = total + slope_x(s, z, sc) * slope_x(q, z, qc)
            total = total + slope_y(sc) * slope_y(qc)
            raw[z] = (0.25 * cp[z + 1]) * total

        rh, rl = halves(raw[...].reshape(cells, ny))
        smooth = (dot(rl, ty[0]) + dot(rh, ty[1])) + dot(rh, ty[0])
        if p % 2 == 0:
            send_depth(p, smooth.reshape(nz, nx, ny))
        else:
            w[p] = smooth.reshape(nz, nx, ny)
            send_tiles(p)

    for p in range(pairs):
        if p % 2 == 0:
            smooth_depth(p, w)
            send_tiles(p)
        else:
            send_depth(p, smooth_tiles(p))
    for p in range(pairs):
        if p % 2 == 0:
            sens[p] = smooth_tiles(p)
        else:
            smooth_depth(p, sens)
        pltpu.make_async_copy(sens.at[p], sens_hbm.at[p], out_sem.at[fields + p]).start()

    for p in range(pairs):
        for d in range(4):
            @pl.when(has[d])
            def _():
                (x_copy if d < 2 else z_copy)(p, d, False).wait_send()
        pltpu.make_async_copy(sens.at[p], sens_hbm.at[p], out_sem.at[fields + p]).wait()
    for f in range(fields):
        pltpu.make_async_copy(
            v.at[end, f, pl.ds(1, nz)], pot_hbm.at[f], out_sem.at[f]
        ).wait()


def local(conductivity, start_fields, electrodes, currents, pair_table, bounds):
    fields, nz, nx, ny = start_fields.shape
    pairs = pair_table.shape[0]
    steps = SWEEPS * DEGREE
    slab = (nz, nx, ny)
    hbm = pl.BlockSpec(memory_space=pl.ANY)
    rim = nz * REACH
    scratch = [
        pltpu.SMEM(pair_table.shape, jnp.int32),
        pltpu.SMEM(bounds.shape, F32),
        pltpu.VMEM(electrodes.shape, jnp.int32),
        pltpu.VMEM(currents.shape, F32),
        pltpu.VMEM((nz + 2, nx, ny), F32),
        pltpu.VMEM((2, fields, nz + 2, nx, ny), F32),
        pltpu.VMEM((fields,) + slab, F32),
        pltpu.VMEM((fields,) + slab, F32),
        pltpu.VMEM((2, fields, 2, nz, 1, ny), F32),
        pltpu.VMEM((fields, 2, nz, 1, ny), F32),
        pltpu.VMEM((2, nz, 1, ny), F32),
        pltpu.VMEM((2, nz, 1, ny), F32),
        pltpu.VMEM((nz + 1, nx, ny), F32),
        pltpu.VMEM(slab, F32),
        pltpu.VMEM(slab, F32),
        pltpu.VMEM(slab, F32),
        pltpu.VMEM(slab, F32),
        pltpu.VMEM(slab, F32),
        pltpu.VMEM(slab, F32),
        pltpu.VMEM((pairs, nz + 2 * REACH, nx, ny), F32),
        pltpu.VMEM((pairs,) + slab, F32),
        pltpu.VMEM((pairs, 2, rim, ny), F32),
        pltpu.VMEM((pairs, 2, rim, ny), F32),
        pltpu.VMEM((pairs,) + slab, F32),
        pltpu.VMEM((steps, 2, 1, ny), F32),
        pltpu.VMEM((2, ny, ny), BF16),
        pltpu.VMEM((2, nz * nx, nz * nx), BF16),
        pltpu.VMEM((2, 2, nz * nx, rim), BF16),
        pltpu.SemaphoreType.DMA((fields + 2,)),
        pltpu.SemaphoreType.DMA((4,)),
        pltpu.SemaphoreType.DMA((fields + pairs,)),
        pltpu.SemaphoreType.DMA((fields, 4)),
        pltpu.SemaphoreType.DMA((2, fields, 4)),
        pltpu.SemaphoreType.DMA((4,)),
        pltpu.SemaphoreType.DMA((4,)),
        pltpu.SemaphoreType.DMA((pairs, 2)),
        pltpu.SemaphoreType.DMA((pairs, 2)),
        pltpu.SemaphoreType.DMA((pairs, 2)),
        pltpu.SemaphoreType.DMA((pairs, 2)),
    ]
    out = jax.ShapeDtypeStruct((fields,) + slab, F32)
    out_sens = jax.ShapeDtypeStruct((pairs,) + slab, F32)
    return pl.pallas_call(
        kernel,
        out_shape=(out, out_sens),
        in_specs=[hbm] * 6,
        out_specs=(hbm, hbm),
        scratch_shapes=scratch,
        compiler_params=pltpu.CompilerParams(
            collective_id=0, has_side_effects=True, vmem_limit_bytes=48 * 1024 * 1024
        ),
    )(pair_table, bounds, electrodes, currents, conductivity, start_fields)


def solution(mesh):
    placed = (P("gz", "xy", None), P(None, "gz", "xy", None), P(), P(), P(), P())
    return jax.shard_map(
        local,
        mesh=mesh,
        in_specs=placed,
        out_specs=(P(None, "gz", "xy", None), P(None, "gz", "xy", None)),
        check_vma=False,
    )
```

```python
import functools
import math

import jax
import jax.numpy as jnp
import ml_dtypes
import numpy as np
from jax import lax
from jax.experimental import pallas as pl
from jax.experimental.pallas import tpu as pltpu
from jax.sharding import PartitionSpec as P

DEGREE = 4
SWEEPS = 2
REACH = 4
MESH = pl.DeviceIdType.MESH
F32 = jnp.float32
BF16 = jnp.bfloat16


def prior_taps():
    raw = [
        (1.0 + math.sqrt(3.0) * k / 2.0) * math.exp(-math.sqrt(3.0) * k / 2.0)
        for k in range(REACH + 1)
    ]
    total = raw[0] + 2.0 * sum(raw[1:])
    return [v / total for v in raw]


def split_taps():
    taps = np.asarray(prior_taps(), np.float32)
    high = taps.astype(ml_dtypes.bfloat16).astype(np.float32)
    return [float(v) for v in high], [float(v) for v in taps - high]


def band(distance, inside=None):
    parts = []
    for taps in split_taps():
        out = jnp.zeros(distance.shape, F32)
        for k in range(REACH + 1):
            hit = jnp.abs(distance) == k
            if inside is not None:
                hit = hit & inside
            out = jnp.where(hit, taps[k], out)
        parts.append(out.astype(BF16))
    return parts


def halves(a):
    high = a.astype(BF16)
    return high, (a - high.astype(F32)).astype(BF16)


def dot(a, b):
    return lax.dot_general(a, b, (((1,), (0,)), ((), ())), preferred_element_type=F32)


def kernel(
    pair_hbm, bounds_hbm, elec_hbm, cur_hbm, cond_hbm, start_hbm, pot_hbm, sens_hbm,
    pair_ref, bounds_ref, elec_ref, cur_ref,
    cp, v, x, r, rowx, sfx, rcx, scx, cz, cxm, cxp, cym, cyp, cd, raw, u, w, xs, xr, sens, coef,
    ty, tc, te,
    load_sem, small_sem, out_sem, send_sem, recv_sem, csend, crecv, zsend, zrecv, xsend, xrecv,
):
    fields, nz, nx, ny = x.shape
    pairs = u.shape[0]
    cells = nz * nx
    ix, iz = lax.axis_index("xy"), lax.axis_index("gz")
    has = [ix > 0, ix < lax.axis_size("xy") - 1, iz > 0, iz < lax.axis_size("gz") - 1]
    place = [
        (ix - 1, iz), (ix + 1, iz), (ix, iz - 1), (ix, iz + 1),
    ]

    barrier = pltpu.get_barrier_semaphore()
    loads = [pltpu.make_async_copy(cond_hbm, cp.at[pl.ds(1, nz)], load_sem.at[0])]
    for f in range(fields):
        loads.append(
            pltpu.make_async_copy(start_hbm.at[f], v.at[0, f, pl.ds(1, nz)], load_sem.at[1 + f])
        )
    loads.append(pltpu.make_async_copy(start_hbm, x, load_sem.at[1 + fields]))
    small = [
        pltpu.make_async_copy(src, dst, small_sem.at[i])
        for i, (src, dst) in enumerate([
            (pair_hbm, pair_ref), (bounds_hbm, bounds_ref), (elec_hbm, elec_ref),
            (cur_hbm, cur_ref),
        ])
    ]
    for copy in loads + small:
        copy.start()

    for d in range(4):
        @pl.when(jnp.logical_not(has[d]))
        def _():
            if d < 2:
                rcx[d] = jnp.zeros(rcx.shape[1:], F32)
                for slot in range(2):
                    for f in range(fields):
                        rowx[slot, f, d] = jnp.zeros(rowx.shape[3:], F32)
                for p in range(pairs):
                    xr[p, d] = jnp.zeros(xr.shape[2:], F32)
            else:
                edge = 0 if d == 2 else nz + 1
                cp[edge] = jnp.zeros((nx, ny), F32)
                for slot in range(2):
                    for f in range(fields):
                        v[slot, f, edge] = jnp.zeros((nx, ny), F32)
                first = 0 if d == 2 else nz + REACH
                for p in range(pairs):
                    u[p, first:first + REACH] = jnp.zeros((REACH, nx, ny), F32)

    for d in range(4):
        @pl.when(has[d])
        def _():
            pl.semaphore_signal(barrier, inc=1, device_id=place[d], device_id_type=MESH)
    pl.semaphore_wait(barrier, sum(h.astype(jnp.int32) for h in has))

    def field_copy(slot, f, d):
        o = d ^ 1
        if d < 2:
            src, dst = sfx.at[f, d], rowx.at[slot, f, o]
        else:
            src = v.at[slot, f, 1 if d == 2 else nz]
            dst = v.at[slot, f, nz + 1 if d == 2 else 0]
        return pltpu.make_async_remote_copy(
            src_ref=src, dst_ref=dst, send_sem=send_sem.at[f, d],
            recv_sem=recv_sem.at[slot, f, o], device_id=place[d], device_id_type=MESH,
        )

    def field_arrival(slot, f, d):
        if d < 2:
            src, dst = sfx.at[f, d], rowx.at[slot, f, d]
        else:
            src = v.at[slot, f, 1 if d == 2 else nz]
            dst = v.at[slot, f, 0 if d == 2 else nz + 1]
        return pltpu.make_async_remote_copy(
            src_ref=src, dst_ref=dst, send_sem=send_sem.at[f, d],
            recv_sem=recv_sem.at[slot, f, d], device_id=place[d], device_id_type=MESH,
        )

    def cond_copy(d, arrives):
        o = d if arrives else d ^ 1
        if d < 2:
            src, dst = scx.at[d], rcx.at[o]
        else:
            src = cp.at[1 if d == 2 else nz]
            dst = cp.at[0 if o == 2 else nz + 1]
        return pltpu.make_async_remote_copy(
            src_ref=src, dst_ref=dst, send_sem=csend.at[d], recv_sem=crecv.at[o],
            device_id=place[d], device_id_type=MESH,
        )

    def send_field(slot, f):
        for d in range(4):
            @pl.when(has[d])
            def _():
                field_copy(slot, f, d).start()

    def wait_field(slot, f):
        for d in range(4):
            @pl.when(has[d])
            def _():
                field_arrival(slot, f, d).wait_recv()
                field_copy(slot, f, d).wait_send()

    loads[0].wait()

    @pl.loop(0, nz)
    def _(z):
        scx[0, z] = cp[z + 1, 0:1, :]
        scx[1, z] = cp[z + 1, nx - 1:nx, :]

    for d in range(4):
        @pl.when(has[d])
        def _():
            cond_copy(d, False).start()
    for f in range(fields):
        loads[1 + f].wait()

        @pl.loop(0, nz)
        def _(z):
            sfx[f, 0, z] = v[0, f, z + 1, 0:1, :]
            sfx[f, 1, z] = v[0, f, z + 1, nx - 1:nx, :]

        send_field(0, f)

    for copy in small:
        copy.wait()

    low = jnp.full((1, ny), bounds_ref[0], F32)
    high = jnp.full((1, ny), bounds_ref[1], F32)
    theta = 0.5 * (low + high)
    delta = 0.5 * (high - low)
    ratio = theta / delta
    for sweep in range(SWEEPS):
        rho = 1.0 / ratio
        for k in range(DEGREE):
            j = sweep * DEGREE + k
            if k == 0:
                coef[j, 0] = jnp.zeros((1, ny), F32)
                coef[j, 1] = 1.0 / theta
            else:
                rho_new = 1.0 / (2.0 * ratio - rho)
                coef[j, 0] = rho_new * rho
                coef[j, 1] = 2.0 * rho_new / delta
                rho = rho_new

    count = cur_ref.shape[1]
    cell_ids = lax.broadcasted_iota(jnp.int32, (cells, count), 0)
    second_ids = lax.broadcasted_iota(jnp.int32, (ny, count), 0)
    for f in range(fields):
        lz = elec_ref[0, f:f + 1, :] - iz * nz
        lx = elec_ref[1, f:f + 1, :] - ix * nx
        inside = (lz >= 0) & (lz < nz) & (lx >= 0) & (lx < nx)
        code = jnp.where(inside, lz * nx + lx, -1)
        at_cell = cell_ids == code
        at_second = jnp.where(second_ids == elec_ref[2, f:f + 1, :], 1.0, 0.0).astype(BF16)
        rest = cur_ref[f:f + 1, :]
        terms = []
        for _ in range(3):
            part = rest.astype(BF16).astype(F32)
            rest = rest - part
            left = jnp.where(at_cell, part, 0.0).astype(BF16)
            terms.append(
                lax.dot_general(
                    left, at_second, (((1,), (1,)), ((), ())), preferred_element_type=F32
                )
            )
        r[f] = ((terms[2] + terms[1]) + terms[0]).reshape(nz, nx, ny)

    a = lax.broadcasted_iota(jnp.int32, (ny, ny), 0)
    b = lax.broadcasted_iota(jnp.int32, (ny, ny), 1)
    ty[0], ty[1] = band(a - b)
    a = lax.broadcasted_iota(jnp.int32, (cells, cells), 0)
    b = lax.broadcasted_iota(jnp.int32, (cells, cells), 1)
    tc[0], tc[1] = band(a % nx - b % nx, a // nx == b // nx)
    rim = nz * REACH
    a = lax.broadcasted_iota(jnp.int32, (cells, rim), 0)
    b = lax.broadcasted_iota(jnp.int32, (cells, rim), 1)
    same = a // nx == b // REACH
    te[0, 0], te[0, 1] = band(a % nx - (b % REACH - REACH), same)
    te[1, 0], te[1, 1] = band(a % nx - (b % REACH + nx), same)

    rows = lax.broadcasted_iota(jnp.int32, (nx, ny), 0)
    lanes = lax.broadcasted_iota(jnp.int32, (nx, ny), 1)

    def x_down(a, row):
        return jnp.where(rows == 0, row, pltpu.roll(a, 1, 0))

    def x_up(a, row):
        return jnp.where(rows == nx - 1, row, pltpu.roll(a, nx - 1, 0))

    for d in range(4):
        @pl.when(has[d])
        def _():
            cond_copy(d, True).wait_recv()
            cond_copy(d, False).wait_send()

    @pl.loop(0, nz, unroll=nz)
    def _(z):
        c = cp[z + 1]
        half = 0.5 * c
        zm = half + 0.5 * cp[z]
        zp = half + 0.5 * cp[z + 2]
        xm = half + 0.5 * x_down(c, rcx[0, z])
        xp = half + 0.5 * x_up(c, rcx[1, z])
        ym = half + 0.5 * jnp.where(lanes == 0, 0.0, pltpu.roll(c, 1, 1))
        yp = half + 0.5 * jnp.where(lanes == ny - 1, 0.0, pltpu.roll(c, ny - 1, 1))
        cz[z] = zm
        cz[z + 1] = zp
        cxm[z] = xm
        cxp[z] = xp
        cym[z] = jnp.where(lanes == 0, 0.0, ym)
        cyp[z] = jnp.where(lanes == ny - 1, 0.0, yp)
        cd[z] = ((zm + zp) + (xm + xp)) + (ym + yp)

    loads[1 + fields].wait()

    def step(j, last):
        slot = lax.rem(j, 2)
        later = 1 - slot
        fac_d = coef[j, 0]
        fac_r = coef[j, 1]
        for f in range(fields):
            wait_field(slot, f)

            @pl.loop(0, nz, unroll=nz)
            def _(z):
                c = v[slot, f, z + 1]
                total = cz[z] * v[slot, f, z] + cz[z + 1] * v[slot, f, z + 2]
                total = total + cxm[z] * x_down(c, rowx[slot, f, 0, z])
                total = total + cxp[z] * x_up(c, rowx[slot, f, 1, z])
                total = total + cym[z] * pltpu.roll(c, 1, 1)
                total = total + cyp[z] * pltpu.roll(c, ny - 1, 1)
                res = r[f, z] + (total - cd[z] * c)
                new = fac_d * c + fac_r * res
                at = x[f, z] + new
                if last:
                    new = at
                else:
                    r[f, z] = res
                    x[f, z] = at
                v[later, f, z + 1] = new
                sfx[f, 0, z] = new[0:1, :]
                sfx[f, 1, z] = new[nx - 1:nx, :]

            send_field(later, f)
            if last:
                pltpu.make_async_copy(
                    v.at[later, f, pl.ds(1, nz)], pot_hbm.at[f], out_sem.at[f]
                ).start()

    steps = SWEEPS * DEGREE
    end = steps % 2

    @pl.loop(0, steps - 1)
    def _(j):
        step(j, False)

    step(jnp.int32(steps - 1), True)

    for f in range(fields):
        wait_field(end, f)

    def z_copy(p, d, arrives):
        o = d if arrives else d ^ 1
        src = u.at[p, pl.ds(REACH if d == 2 else nz, REACH)]
        dst = u.at[p, pl.ds(0 if o == 2 else nz + REACH, REACH)]
        return pltpu.make_async_remote_copy(
            src_ref=src, dst_ref=dst, send_sem=zsend.at[p, d - 2], recv_sem=zrecv.at[p, o - 2],
            device_id=place[d], device_id_type=MESH,
        )

    def x_copy(p, d, arrives):
        o = d if arrives else d ^ 1
        return pltpu.make_async_remote_copy(
            src_ref=xs.at[p, d], dst_ref=xr.at[p, o], send_sem=xsend.at[p, d],
            recv_sem=xrecv.at[p, o], device_id=place[d], device_id_type=MESH,
        )

    def slope_x(f, z, c):
        return x_up(c, rowx[end, f, 1, z]) - x_down(c, rowx[end, f, 0, z])

    def slope_y(c):
        ahead = jnp.where(lanes == ny - 1, 0.0, pltpu.roll(c, ny - 1, 1))
        return ahead - jnp.where(lanes == 0, 0.0, pltpu.roll(c, 1, 1))

    def send_depth(p, values):
        u[p, REACH:REACH + nz] = values
        for d in (2, 3):
            @pl.when(has[d])
            def _():
                z_copy(p, d, False).start()

    def send_tiles(p):
        for z in range(nz):
            values = w[p, z]
            xs[p, 0, z * REACH:(z + 1) * REACH] = values[0:REACH]
            xs[p, 1, z * REACH:(z + 1) * REACH] = values[nx - REACH:nx]
        for d in (0, 1):
            @pl.when(has[d])
            def _():
                x_copy(p, d, False).start()

    taps = prior_taps()

    def smooth_depth(p, out):
        for d in (2, 3):
            @pl.when(has[d])
            def _():
                z_copy(p, d, True).wait_recv()
        for z in range(nz):
            total = taps[0] * u[p, z + REACH]
            for k in range(1, REACH + 1):
                total = total + taps[k] * (u[p, z + REACH - k] + u[p, z + REACH + k])
            out[p, z] = total

    def smooth_tiles(p):
        wh, wl = halves(w[p].reshape(cells, ny))
        total = (dot(tc[0], wl) + dot(tc[1], wh)) + dot(tc[0], wh)
        for d in (0, 1):
            @pl.when(has[d])
            def _():
                x_copy(p, d, True).wait_recv()
        for d in (0, 1):
            eh, el = halves(xr[p, d])
            total = total + ((dot(te[d, 0], el) + dot(te[d, 1], eh)) + dot(te[d, 0], eh))
        return total.reshape(nz, nx, ny)

    for p in range(pairs):
        s = pair_ref[p, 0]
        q = pair_ref[p, 1] + 2

        @pl.loop(0, nz, unroll=nz)
        def _(z):
            sc = v[end, s, z + 1]
            qc = v[end, q, z + 1]
            total = (v[end, s, z + 2] - v[end, s, z]) * (v[end, q, z + 2] - v[end, q, z])
            total = total + slope_x(s, z, sc) * slope_x(q, z, qc)
            total = total + slope_y(sc) * slope_y(qc)
            raw[z] = (0.25 * cp[z + 1]) * total

        rh, rl = halves(raw[...].reshape(cells, ny))
        smooth = (dot(rl, ty[0]) + dot(rh, ty[1])) + dot(rh, ty[0])
        if p % 2 == 0:
            send_depth(p, smooth.reshape(nz, nx, ny))
        else:
            w[p] = smooth.reshape(nz, nx, ny)
            send_tiles(p)

    for p in range(pairs):
        if p % 2 == 0:
            smooth_depth(p, w)
            send_tiles(p)
        else:
            send_depth(p, smooth_tiles(p))
    for p in range(pairs):
        if p % 2 == 0:
            sens[p] = smooth_tiles(p)
        else:
            smooth_depth(p, sens)
        pltpu.make_async_copy(sens.at[p], sens_hbm.at[p], out_sem.at[fields + p]).start()

    for p in range(pairs):
        for d in range(4):
            @pl.when(has[d])
            def _():
                (x_copy if d < 2 else z_copy)(p, d, False).wait_send()
        pltpu.make_async_copy(sens.at[p], sens_hbm.at[p], out_sem.at[fields + p]).wait()
    for f in range(fields):
        pltpu.make_async_copy(
            v.at[end, f, pl.ds(1, nz)], pot_hbm.at[f], out_sem.at[f]
        ).wait()


def local(conductivity, start_fields, electrodes, currents, pair_table, bounds):
    fields, nz, nx, ny = start_fields.shape
    pairs = pair_table.shape[0]
    steps = SWEEPS * DEGREE
    slab = (nz, nx, ny)
    hbm = pl.BlockSpec(memory_space=pl.ANY)
    rim = nz * REACH
    scratch = [
        pltpu.SMEM(pair_table.shape, jnp.int32),
        pltpu.SMEM(bounds.shape, F32),
        pltpu.VMEM(electrodes.shape, jnp.int32),
        pltpu.VMEM(currents.shape, F32),
        pltpu.VMEM((nz + 2, nx, ny), F32),
        pltpu.VMEM((2, fields, nz + 2, nx, ny), F32),
        pltpu.VMEM((fields,) + slab, F32),
        pltpu.VMEM((fields,) + slab, F32),
        pltpu.VMEM((2, fields, 2, nz, 1, ny), F32),
        pltpu.VMEM((fields, 2, nz, 1, ny), F32),
        pltpu.VMEM((2, nz, 1, ny), F32),
        pltpu.VMEM((2, nz, 1, ny), F32),
        pltpu.VMEM((nz + 1, nx, ny), F32),
        pltpu.VMEM(slab, F32),
        pltpu.VMEM(slab, F32),
        pltpu.VMEM(slab, F32),
        pltpu.VMEM(slab, F32),
        pltpu.VMEM(slab, F32),
        pltpu.VMEM(slab, F32),
        pltpu.VMEM((pairs, nz + 2 * REACH, nx, ny), F32),
        pltpu.VMEM((pairs,) + slab, F32),
        pltpu.VMEM((pairs, 2, rim, ny), F32),
        pltpu.VMEM((pairs, 2, rim, ny), F32),
        pltpu.VMEM((pairs,) + slab, F32),
        pltpu.VMEM((steps, 2, 1, ny), F32),
        pltpu.VMEM((2, ny, ny), BF16),
        pltpu.VMEM((2, nz * nx, nz * nx), BF16),
        pltpu.VMEM((2, 2, nz * nx, rim), BF16),
        pltpu.SemaphoreType.DMA((fields + 2,)),
        pltpu.SemaphoreType.DMA((4,)),
        pltpu.SemaphoreType.DMA((fields + pairs,)),
        pltpu.SemaphoreType.DMA((fields, 4)),
        pltpu.SemaphoreType.DMA((2, fields, 4)),
        pltpu.SemaphoreType.DMA((4,)),
        pltpu.SemaphoreType.DMA((4,)),
        pltpu.SemaphoreType.DMA((pairs, 2)),
        pltpu.SemaphoreType.DMA((pairs, 2)),
        pltpu.SemaphoreType.DMA((pairs, 2)),
        pltpu.SemaphoreType.DMA((pairs, 2)),
    ]
    out = jax.ShapeDtypeStruct((fields,) + slab, F32)
    out_sens = jax.ShapeDtypeStruct((pairs,) + slab, F32)
    return pl.pallas_call(
        kernel,
        out_shape=(out, out_sens),
        in_specs=[hbm] * 6,
        out_specs=(hbm, hbm),
        scratch_shapes=scratch,
        compiler_params=pltpu.CompilerParams(
            collective_id=0, has_side_effects=True, vmem_limit_bytes=62 * 1024 * 1024
        ),
    )(pair_table, bounds, electrodes, currents, conductivity, start_fields)


def solution(mesh):
    placed = (P("gz", "xy", None), P(None, "gz", "xy", None), P(), P(), P(), P())
    return jax.shard_map(
        local,
        mesh=mesh,
        in_specs=placed,
        out_specs=(P(None, "gz", "xy", None), P(None, "gz", "xy", None)),
        check_vma=False,
    )
```
